32 devices in a mesh: tm: 8 (over y, x, core), row: 4 (over z).
Axes of the slice: x: 2, y: 2, z: 4, core: 2. Of those that a mesh axis runs over, the one named last changes fastest.
Arguments:
- latent: bfloat16 [16, 8, 40, 2240], P('tm', 'row'), may hold values from -6 to 6
- query_raw: bfloat16 [16, 8, 40, 2240], P('tm', 'row'), may hold values from -6 to 6
- key_raw: bfloat16 [16, 8, 40, 2240], P('tm', 'row'), may hold values from -12 to 12
- value_raw: bfloat16 [16, 8, 40, 2240], P('tm', 'row'), may hold values from -12 to 12
- query_gain: float32 [2240], replicated, may hold values from 0.4 to 2.5
- key_gain: float32 [2240], replicated, may hold values from 0.4 to 2.5
- space_kernel: float32 [3, 3, 2240], replicated, may hold values from -2 to 2
- time_kernel: float32 [3, 2240], replicated, may hold values from -3.5 to 3.5
- first_weight: bfloat16 [2240, 2048], P('tm', 'row'), may hold values from -0.125 to 0.125
- first_bias: float32 [2048], replicated, may hold values from -3 to 3
- second_weight: bfloat16 [2048, 1280], P('row', 'tm'), may hold values from -0.125 to 0.125
- second_bias: float32 [1280], replicated, may hold values from -3 to 3
- target_keys: bfloat16 [16, 256, 1280], P('tm', 'row'), may hold values from -410 to 410
- target_values: bfloat16 [16, 256, 1280], P('tm', 'row'), may hold values from -12 to 12
Outputs:
- blended: bfloat16 [16, 8, 40, 2240], P('tm', 'row')
- attended: bfloat16 [16, 8, 40, 1280], P('tm', 'row')
The draws below stay inside these ranges and needn't reach their ends.
All inputs are finite; a program needn't handle non-finite values.
Results may differ from the reference program's by a relative error of at most 0.01545.
The reference program's roundings to bfloat16 on the way count: a program that leaves them out, or rounds other values in their place, can miss the bound.
Values may be sent and summed in bfloat16 or wider, within the bound.
A program may use at most 128 MiB of HBM per device.

```python
import math
import jax
import jax.numpy as jnp
from jax import lax

HEADS = 70
HEAD_DIM = 32
D = 2240
PROJ = 2048
AHEADS = 16
AHEAD_DIM = 80
OUTF = 1280
TGT = 256
COLS = 40
BLOCK_FRAMES = 2
FRAMES = 16
HEIGHT = 8


def paired_fields(key):
    base_key = jax.random.fold_in(key, 11)
    key_noise_key = jax.random.fold_in(base_key, 0)
    value_noise_key = jax.random.fold_in(base_key, 1)
    key_offset_key = jax.random.fold_in(base_key, 2)
    value_offset_key = jax.random.fold_in(base_key, 3)
    coef_key = jax.random.fold_in(base_key, 5)
    sign_key = jax.random.fold_in(base_key, 6)
    frame_key = jax.random.fold_in(base_key, 7)
    shape = (FRAMES, HEIGHT, COLS, D)
    key_noise = jax.random.normal(key_noise_key, shape, jnp.float32)
    value_noise = jax.random.normal(value_noise_key, shape, jnp.float32)
    spread = jnp.full((FRAMES, HEIGHT, 1, 1), 1.5, jnp.float32)
    key_offsets = spread * jax.random.normal(key_offset_key, (FRAMES, HEIGHT, 1, D), jnp.float32)
    value_offsets = spread * jax.random.normal(value_offset_key, (FRAMES, HEIGHT, 1, D), jnp.float32)
    magnitude = jax.random.uniform(coef_key, (D,), jnp.float32, 1.5, 3.0)
    signs = jnp.where(jax.random.uniform(sign_key, (D,), jnp.float32) < 0.5, -1.0, 1.0)
    frame_factor = jnp.exp(jax.random.uniform(frame_key, (FRAMES, 1, 1, 1), jnp.float32, math.log(0.6), math.log(1.6)))
    rolled = jnp.roll(key_noise.reshape(FRAMES, HEIGHT, COLS, HEADS, HEAD_DIM), 1, axis=-1).reshape(shape)
    keys_drawn = jnp.clip(key_noise + key_offsets, -12.0, 12.0).astype(jnp.bfloat16)
    values_drawn = jnp.clip(frame_factor * magnitude * signs * rolled + value_noise + value_offsets, -12.0, 12.0).astype(jnp.bfloat16)
    return (keys_drawn, values_drawn)


def draw_key_raw(key, part):
    return paired_fields(key)[0]


def draw_value_raw(key, part):
    return paired_fields(key)[1]


def draw_target_keys(key, part):
    base_key = jax.random.fold_in(jax.random.fold_in(key, 37), 0)
    shape = (FRAMES, TGT, OUTF)
    keys_drawn = jnp.clip(3.0 * jax.random.normal(base_key, shape, jnp.float32), -15.0, 15.0)
    return keys_drawn.astype(jnp.bfloat16)


def steps_of(key, extent, cuts, smallest, largest):
    def one(axis_at, shards_of):
        draws = jax.random.uniform(jax.random.fold_in(jax.random.fold_in(key, 6), axis_at), (shards_of,), jnp.float32, smallest / len(cuts), largest / len(cuts))
        return jnp.repeat(jnp.exp(draws), extent[axis_at] // shards_of).reshape((-1,) + (1,) * (len(extent) - axis_at - 1))

    gain = one(*cuts[0])
    for cut in cuts[1:]:
        gain = gain * one(*cut)
    return gain


def bell_draw(stream_key, extent, scale, reach, cuts=(), held_as=jnp.bfloat16):
    values = scale * jax.random.normal(stream_key, extent, jnp.float32)
    if cuts:
        values = values * steps_of(stream_key, extent, cuts, -0.22, 0.18)
    return jnp.clip(values, -reach, reach).astype(held_as)


def setup_inputs(seed: int = 0) -> dict:
    streams_of = jax.random.split(jax.random.key(seed), 15)
    latent = bell_draw(streams_of[0], (FRAMES, HEIGHT, COLS, D), 1.0, 6.0, ((0, 8), (1, 4)))
    query_raw = bell_draw(streams_of[1], (FRAMES, HEIGHT, COLS, D), 1.0, 6.0, ((0, 8), (1, 4)))
    key_raw = draw_key_raw(jax.random.fold_in(streams_of[14], 71), 0)
    value_raw = draw_value_raw(jax.random.fold_in(streams_of[14], 71), 0)
    query_gain = jnp.clip(jnp.exp(jax.random.uniform(streams_of[4], (D,), jnp.float32, math.log(0.4), math.log(2.5))), 0.4, 2.5)
    key_gain = jnp.clip(jnp.exp(jax.random.uniform(streams_of[5], (D,), jnp.float32, math.log(0.4), math.log(2.5))), 0.4, 2.5)
    space_kernel = bell_draw(streams_of[6], (3, 3, D), 9 ** -0.5, 2.0, (), jnp.float32)
    time_kernel = bell_draw(streams_of[7], (3, D), 3 ** -0.5, 3.5, (), jnp.float32)
    first_weight = bell_draw(streams_of[8], (D, PROJ), D ** -0.5, 0.125, ((0, 8), (1, 4)))
    first_bias = bell_draw(streams_of[9], (PROJ,), 0.5, 3.0, (), jnp.float32)
    second_weight = bell_draw(streams_of[10], (PROJ, OUTF), PROJ ** -0.5, 0.125, ((0, 4), (1, 8)))
    second_bias = bell_draw(streams_of[11], (OUTF,), 0.5, 3.0, (), jnp.float32)
    target_keys = draw_target_keys(jax.random.fold_in(streams_of[14], 71), 0)
    target_values = bell_draw(streams_of[13], (FRAMES, TGT, OUTF), 2.0, 12.0, ((0, 8), (1, 4)))
    return {"latent": latent, "query_raw": query_raw, "key_raw": key_raw, "value_raw": value_raw, "query_gain": query_gain, "key_gain": key_gain, "space_kernel": space_kernel, "time_kernel": time_kernel, "first_weight": first_weight, "first_bias": first_bias, "second_weight": second_weight, "second_bias": second_bias, "target_keys": target_keys, "target_values": target_values}


def head_features(source, scaling):
    values = source.astype(jnp.float32).reshape(source.shape[:-1] + (HEADS, HEAD_DIM))
    mean_square = jnp.maximum(lax.optimization_barrier(jnp.mean(values * values, axis=-1, keepdims=True)), 0.25)
    return jax.nn.relu(values * lax.rsqrt(mean_square) * scaling.reshape(HEADS, HEAD_DIM))

def frame_softmax(query_split, key_split, value_split):
    score_scale = 1.0 / AHEAD_DIM ** 0.5
    scores = jnp.einsum('cqgd,ckgd->cgqk', query_split.astype(jnp.float32), key_split.astype(jnp.float32), precision=lax.Precision.HIGHEST) * score_scale
    row_max = lax.optimization_barrier(jnp.max(scores, axis=-1, keepdims=True))
    weights = jnp.exp(scores - row_max)
    row_total = lax.optimization_barrier(jnp.sum(weights, axis=-1))
    weights_low = lax.optimization_barrier(weights.astype(jnp.bfloat16))
    result = jnp.einsum('cgqk,ckgd->cqgd', weights_low.astype(jnp.float32), value_split.astype(jnp.float32), precision=lax.Precision.HIGHEST)
    return result / jnp.transpose(row_total, (0, 2, 1))[..., None]

def reference(latent, query_raw, key_raw, value_raw, query_gain, key_gain, space_kernel, time_kernel, first_weight, first_bias, second_weight, second_bias, target_keys, target_values):
    block_count = FRAMES // BLOCK_FRAMES

    def shaped(source):
        return source.reshape((block_count, BLOCK_FRAMES) + source.shape[1:])

    def block_sums(inputs):
        key_part, value_part = inputs
        key_feat = head_features(key_part, key_gain)
        value_feat = value_part.astype(jnp.float32).reshape(key_feat.shape)
        key_state = jnp.einsum('crwhd,crwhe->dhe', key_feat, value_feat, precision=lax.Precision.HIGHEST).reshape(HEAD_DIM, D)
        return (key_state, lax.optimization_barrier(jnp.sum(key_feat, axis=(0, 1, 2))).reshape(D))
    states, keysums = lax.map(block_sums, (shaped(key_raw), shaped(value_raw)))
    states = jnp.cumsum(states, axis=0)
    keysums = jnp.cumsum(keysums, axis=0)

    def attend(inputs):
        query_part, residue, key_state, key_total = inputs
        query_feat = head_features(query_part, query_gain)
        numerator = jnp.einsum('crwhd,dhe->crwhe', query_feat, key_state.reshape(HEAD_DIM, HEADS, HEAD_DIM), precision=lax.Precision.HIGHEST)
        denominator = jnp.einsum('crwhd,hd->crwh', query_feat, key_total.reshape(HEADS, HEAD_DIM), precision=lax.Precision.HIGHEST) + 1e-06
        linear_out = (numerator / denominator[..., None]).reshape(residue.shape)
        return (residue.astype(jnp.float32) + linear_out).astype(jnp.bfloat16)
    hidden_in = lax.map(attend, (shaped(query_raw), shaped(latent), states, keysums)).reshape(latent.shape)
    padded = jnp.pad(hidden_in, ((1, 1), (1, 1), (1, 1), (0, 0)))

    def finish(inputs):
        position, key_part, value_part = inputs
        first_frame = (position * BLOCK_FRAMES).astype(jnp.int32)
        anchor = jnp.zeros((), jnp.int32)
        window = lax.dynamic_slice(padded, (first_frame, anchor, anchor, anchor), (BLOCK_FRAMES + 2, HEIGHT + 2, COLS + 2, D))
        center = window[1:-1, 1:-1, 1:-1].astype(jnp.float32)
        spatial = jnp.zeros(center.shape, jnp.float32)
        for shift_row in range(3):
            for shift_col in range(3):
                spatial = spatial + space_kernel[shift_row, shift_col] * window[1:-1, shift_row:shift_row + HEIGHT, shift_col:shift_col + COLS].astype(jnp.float32)
        temporal = jnp.zeros(center.shape, jnp.float32)
        for shift_time in range(3):
            temporal = temporal + time_kernel[shift_time] * window[shift_time:shift_time + BLOCK_FRAMES, 1:-1, 1:-1].astype(jnp.float32)
        blended = (center + spatial + temporal).astype(jnp.bfloat16)
        tokens = blended.reshape(-1, D)
        hidden_units = jax.nn.silu(jnp.dot(tokens, first_weight, preferred_element_type=jnp.float32) + first_bias).astype(jnp.bfloat16)
        queries = (jnp.dot(hidden_units, second_weight, preferred_element_type=jnp.float32) + second_bias).astype(jnp.bfloat16)
        query_split = queries.reshape(BLOCK_FRAMES, HEIGHT * COLS, AHEADS, AHEAD_DIM)
        key_split = key_part.reshape(BLOCK_FRAMES, TGT, AHEADS, AHEAD_DIM)
        value_split = value_part.reshape(BLOCK_FRAMES, TGT, AHEADS, AHEAD_DIM)
        result = frame_softmax(query_split, key_split, value_split)
        return (blended, result.reshape(BLOCK_FRAMES, HEIGHT, COLS, OUTF).astype(jnp.bfloat16))
    blended, attended = lax.map(finish, (jnp.arange(block_count), shaped(target_keys), shaped(target_values)))
    return (blended.reshape(latent.shape), attended.reshape(FRAMES, HEIGHT, COLS, OUTF))
```

```python
import functools

import jax
import jax.numpy as jnp
from jax import lax
from jax.experimental import pallas as pl
from jax.experimental.pallas import tpu as pltpu
from jax.sharding import PartitionSpec as P

HEADS = 70
HEAD_DIM = 32
AHEADS = 16
AHEAD_DIM = 80
LANES = 128
SLAB = 48
STATE_TYPE = jnp.float32
F32, BF16 = jnp.float32, jnp.bfloat16
MESH = pl.DeviceIdType.MESH


def groups_of(width):
    return [(start, min(LANES, width - start)) for start in range(0, width, LANES)]


def same_head(size):
    row = lax.broadcasted_iota(jnp.int32, (size, size), 0) // HEAD_DIM
    col = lax.broadcasted_iota(jnp.int32, (size, size), 1) // HEAD_DIM
    return (row == col).astype(F32)


def parts(value):
    high = value.astype(BF16)
    return high, (value - high.astype(F32)).astype(BF16)


def dot(left, right):
    return jnp.dot(left, right, preferred_element_type=F32)


def token_dot(left, right):
    return lax.dot_general(left, right, (((0,), (0,)), ((), ())), preferred_element_type=F32)


def head_sums(value, ones):
    high, low = parts(value)
    return dot(high, ones) + dot(low, ones)


def features(source, gain, ones):
    values = source.astype(F32)
    mean_square = jnp.maximum(head_sums(values * values, ones) * (1.0 / HEAD_DIM), 0.25)
    return jnp.maximum(values * lax.rsqrt(mean_square) * gain, 0.0)


def front_kernel(
    count_t, count_r, frames, rows, cols,
    key_ref, value_ref, query_ref, latent_ref, key_gain, query_gain, space_ref, time_ref,
    out_ref,
    state, row_in, mine, before, final, hidden,
    rs_send, rs_recv, p_send, p_recv, g_send, g_recv, h_send, h_recv,
):
    me_t, me_r = lax.axis_index("tm"), lax.axis_index("row")
    width = key_ref.shape[1]
    groups = groups_of(width)
    per_part = -(-len(groups) // count_r)

    barrier = pltpu.get_barrier_semaphore()

    def greet_t(k, carry):
        pl.semaphore_signal(
            barrier, inc=1, device_id={"tm": lax.rem(me_t + k, count_t)}, device_id_type=MESH
        )
        return carry

    lax.fori_loop(1, count_t, greet_t, 0)
    for k in range(1, count_r):
        pl.semaphore_signal(
            barrier, inc=1, device_id={"row": lax.rem(me_r + k, count_r)}, device_id_type=MESH
        )

    state[...] = jnp.zeros_like(state)
    for index, (start, size) in enumerate(groups):
        mask = same_head(size)
        ones = mask.astype(BF16)
        lanes = pl.ds(start, size)
        feat = features(key_ref[:, lanes], key_gain[:, lanes], ones)
        high, low = parts(feat)
        values = value_ref[:, lanes]
        outer = (token_dot(high, values) + token_dot(low, values)) * mask
        packed = outer[0:HEAD_DIM]
        for head in range(1, size // HEAD_DIM):
            packed = packed + outer[head * HEAD_DIM : (head + 1) * HEAD_DIM]
        sums = jnp.broadcast_to(jnp.sum(feat, axis=0, keepdims=True), (SLAB - HEAD_DIM, size))
        tail = lax.broadcasted_iota(jnp.int32, sums.shape, 0) == 0
        block = jnp.concatenate([packed, jnp.where(tail, sums, 0.0)], axis=0)
        state[index // per_part, :, pl.ds((index % per_part) * LANES, size)] = block.astype(
            STATE_TYPE
        )

    pl.semaphore_wait(barrier, count_t - 1 + count_r - 1)

    def row_copy(peer, slot):
        return pltpu.make_async_remote_copy(
            src_ref=state.at[peer], dst_ref=row_in.at[slot],
            send_sem=rs_send.at[peer], recv_sem=rs_recv.at[slot],
            device_id={"row": peer}, device_id_type=MESH,
        )

    for k in range(1, count_r):
        row_copy(lax.rem(me_r + k, count_r), me_r).start()
    total = state[me_r].astype(F32)
    for k in range(1, count_r):
        peer = lax.rem(me_r + k, count_r)
        row_copy(peer, peer).wait_recv()
        total = total + row_in[peer].astype(F32)
    mine[...] = total.astype(STATE_TYPE)

    def prefix_copy(peer, slot):
        return pltpu.make_async_remote_copy(
            src_ref=mine, dst_ref=before.at[slot],
            send_sem=p_send.at[peer], recv_sem=p_recv.at[slot],
            device_id={"tm": peer}, device_id_type=MESH,
        )

    def send_later(peer, carry):
        prefix_copy(peer, me_t).start()
        return carry

    lax.fori_loop(me_t + 1, count_t, send_later, 0)
    final[me_r] = total.astype(STATE_TYPE)

    def add_earlier(peer, carry):
        prefix_copy(peer, peer).wait_recv()
        final[me_r] = (final[me_r].astype(F32) + before[peer].astype(F32)).astype(STATE_TYPE)
        return carry

    lax.fori_loop(0, me_t, add_earlier, 0)

    def final_copy(peer, slot):
        return pltpu.make_async_remote_copy(
            src_ref=final.at[me_r], dst_ref=final.at[slot],
            send_sem=g_send.at[peer], recv_sem=g_recv.at[slot],
            device_id={"row": peer}, device_id_type=MESH,
        )

    def final_arrival(peer):
        return pltpu.make_async_remote_copy(
            src_ref=final.at[peer], dst_ref=final.at[peer],
            send_sem=g_send.at[peer], recv_sem=g_recv.at[peer],
            device_id={"row": peer}, device_id_type=MESH,
        )

    for k in range(1, count_r):
        final_copy(lax.rem(me_r + k, count_r), me_r).start()
    for k in range(1, count_r):
        final_arrival(lax.rem(me_r + k, count_r)).wait_recv()

    for index, (start, size) in enumerate(groups):
        mask = same_head(size)
        ones = mask.astype(BF16)
        lanes = pl.ds(start, size)
        held = final[index // per_part, :, pl.ds((index % per_part) * LANES, size)].astype(F32)
        feat = features(query_ref[:, lanes], query_gain[:, lanes], ones)
        high, low = parts(feat)
        table = jnp.concatenate([held[0:HEAD_DIM]] * (size // HEAD_DIM), axis=0) * mask
        table_high, table_low = parts(table)
        numerator = dot(high, table_high) + dot(low, table_high) + dot(high, table_low)
        denominator = head_sums(feat * held[HEAD_DIM : HEAD_DIM + 1], ones) + 1e-06
        mixed = latent_ref[:, lanes].astype(F32) + numerator / denominator
        for f in range(frames):
            for r in range(rows):
                at = (f * rows + r) * cols
                padded = jnp.concatenate(
                    [mixed[at : at + cols], jnp.zeros((SLAB - cols, size), F32)], axis=0
                )
                hidden[f + 1, r + 1, :, lanes] = padded.astype(BF16)

    body_f, body_r = pl.ds(1, frames), pl.ds(1, rows)
    moves = (
        ("tm", me_t, count_t, -1, hidden.at[1, body_r], hidden.at[frames + 1, body_r]),
        ("tm", me_t, count_t, 1, hidden.at[frames, body_r], hidden.at[0, body_r]),
        ("row", me_r, count_r, -1, hidden.at[body_f, 1], hidden.at[body_f, rows + 1]),
        ("row", me_r, count_r, 1, hidden.at[body_f, rows], hidden.at[body_f, 0]),
    )

    def halo(i):
        axis, me, count, step, source, target = moves[i]
        return pltpu.make_async_remote_copy(
            src_ref=source, dst_ref=target, send_sem=h_send.at[i], recv_sem=h_recv.at[i],
            device_id={axis: lax.rem(me + step + count, count)}, device_id_type=MESH,
        )

    def sends(i):
        _, me, count, step, _, _ = moves[i]
        return (me > 0) if step < 0 else (me < count - 1)

    def receives(i):
        _, me, count, step, _, _ = moves[i]
        return (me < count - 1) if step < 0 else (me > 0)

    for i in range(4):
        pl.when(sends(i))(halo(i).start)
    for i in range(4):
        target = moves[i][5]

        @pl.when(jnp.logical_not(receives(i)))
        def _():
            target[...] = jnp.zeros(target.shape, BF16)

    for i in range(4):
        pl.when(receives(i))(halo(i).wait_recv)

    for start, size in groups:
        lanes = pl.ds(start, size)
        taps = [space_ref[i : i + 1, lanes] for i in range(9)]
        times = [time_ref[i : i + 1, lanes] for i in range(3)]
        for f in range(frames):
            for r in range(rows):
                total = jnp.zeros((SLAB, size), F32)
                for a in range(3):
                    slab = hidden[f + 1, r + a, :, lanes].astype(F32)
                    if a == 1:
                        total = total + slab * (1.0 + times[1])
                    total = total + taps[3 * a + 1] * slab
                    total = total + taps[3 * a] * pltpu.roll(slab, 1, 0)
                    total = total + taps[3 * a + 2] * pltpu.roll(slab, SLAB - 1, 0)
                for a in (0, 2):
                    total = total + times[a] * hidden[f + a, r + 1, :, lanes].astype(F32)
                out_ref[f * rows + r, :, lanes] = total[0:cols].astype(BF16)

    for i in range(4):
        pl.when(sends(i))(halo(i).wait_send)
    for k in range(1, count_r):
        peer = lax.rem(me_r + k, count_r)
        row_copy(peer, me_r).wait_send()
        final_copy(peer, me_r).wait_send()

    def sent(peer, carry):
        prefix_copy(peer, me_t).wait_send()
        return carry

    lax.fori_loop(me_t + 1, count_t, sent, 0)


def front(latent, query_raw, key_raw, value_raw, query_gain, key_gain, space_kernel, time_kernel):
    frames, rows, cols, width = latent.shape
    count_t, count_r = lax.axis_size("tm"), lax.axis_size("row")
    tokens = frames * rows * cols
    part = -(-len(groups_of(width)) // count_r) * LANES
    flat = lambda x: x.reshape(tokens, width)
    dma = pltpu.SemaphoreType.DMA
    vmem = pl.BlockSpec(memory_space=pltpu.VMEM)
    out = pl.pallas_call(
        functools.partial(front_kernel, count_t, count_r, frames, rows, cols),
        out_shape=jax.ShapeDtypeStruct((frames * rows, cols, width), BF16),
        in_specs=[vmem] * 8,
        out_specs=vmem,
        scratch_shapes=[
            pltpu.VMEM((count_r, SLAB, part), STATE_TYPE),
            pltpu.VMEM((count_r, SLAB, part), STATE_TYPE),
            pltpu.VMEM((SLAB, part), STATE_TYPE),
            pltpu.VMEM((count_t, SLAB, part), STATE_TYPE),
            pltpu.VMEM((count_r, SLAB, part), STATE_TYPE),
            pltpu.VMEM((frames + 2, rows + 2, SLAB, width), BF16),
            dma((count_r,)), dma((count_r,)), dma((count_t,)), dma((count_t,)),
            dma((count_r,)), dma((count_r,)), dma((4,)), dma((4,)),
        ],
        compiler_params=pltpu.CompilerParams(
            collective_id=0, has_side_effects=True, vmem_limit_bytes=40 * 1024 * 1024
        ),
    )(
        flat(key_raw), flat(value_raw), flat(query_raw), flat(latent),
        key_gain.reshape(1, width), query_gain.reshape(1, width),
        space_kernel.reshape(9, width), time_kernel,
    )
    return out.reshape(latent.shape)


def per_device(
    latent, query_raw, key_raw, value_raw, query_gain, key_gain, space_kernel, time_kernel,
    first_weight, first_bias, second_weight, second_bias, target_keys, target_values,
):
    frames, rows, cols, width = latent.shape
    blended = front(
        latent, query_raw, key_raw, value_raw, query_gain, key_gain, space_kernel, time_kernel
    )
    gather = functools.partial(lax.all_gather, tiled=True)
    first_full = gather(gather(first_weight, "row", axis=1), "tm", axis=0)
    second_full = gather(gather(second_weight, "row", axis=0), "tm", axis=1)
    keys, values = (gather(x, "row", axis=1) for x in (target_keys, target_values))
    tokens = blended.reshape(-1, width)
    units = jax.nn.silu(dot(tokens, first_full) + first_bias).astype(BF16)
    queries = (dot(units, second_full) + second_bias).astype(BF16)
    split = lambda x: x.reshape(frames, -1, AHEADS, AHEAD_DIM)
    scores = jnp.einsum(
        "cqgd,ckgd->cgqk", split(queries), split(keys), preferred_element_type=F32
    ) * (1.0 / AHEAD_DIM**0.5)
    weights = jnp.exp(scores - jnp.max(scores, axis=-1, keepdims=True))
    row_total = jnp.sum(weights, axis=-1)
    result = jnp.einsum(
        "cgqk,ckgd->cqgd", weights.astype(BF16), split(values), preferred_element_type=F32
    )
    result = result / jnp.transpose(row_total, (0, 2, 1))[..., None]
    attended = result.astype(BF16).reshape(frames, rows, cols, -1)
    return (blended, attended)


def solution(mesh):
    tokens = P("tm", "row", None, None)
    targets = P("tm", "row", None)
    return jax.shard_map(
        per_device,
        mesh=mesh,
        in_specs=(
            tokens, tokens, tokens, tokens, P(), P(), P(), P(),
            P("tm", "row"), P(), P("row", "tm"), P(), targets, targets,
        ),
        out_specs=(tokens, tokens),
        check_vma=False,
    )
```

```python
import functools

import jax
import jax.numpy as jnp
from jax import lax
from jax.experimental import pallas as pl
from jax.experimental.pallas import tpu as pltpu
from jax.sharding import PartitionSpec as P

HEADS = 70
HEAD_DIM = 32
AHEADS = 16
AHEAD_DIM = 80
LANES = 128
SLAB = 48
HELD_BEHIND = 22
CUBE = 8
STATE_TYPE = jnp.float32
F32, BF16 = jnp.float32, jnp.bfloat16
MESH = pl.DeviceIdType.MESH


def groups_of(width):
    return [(start, min(LANES, width - start)) for start in range(0, width, LANES)]


def same_head(size):
    row = lax.broadcasted_iota(jnp.int32, (size, size), 0) // HEAD_DIM
    col = lax.broadcasted_iota(jnp.int32, (size, size), 1) // HEAD_DIM
    return (row == col).astype(F32)


def parts(value):
    high = value.astype(BF16)
    return high, (value - high.astype(F32)).astype(BF16)


def dot(left, right):
    return jnp.dot(left, right, preferred_element_type=F32)


def token_dot(left, right):
    return lax.dot_general(left, right, (((0,), (0,)), ((), ())), preferred_element_type=F32)


def head_sums(value, ones):
    high, low = parts(value)
    return dot(high, ones) + dot(low, ones)


def features(source, gain, ones):
    values = source.astype(F32)
    mean_square = jnp.maximum(head_sums(values * values, ones) * (1.0 / HEAD_DIM), 0.25)
    return jnp.maximum(values * lax.rsqrt(mean_square) * gain, 0.0)


def front_kernel(
    count_t, count_r, frames, rows, cols,
    key_ref, value_ref, query_ref, latent_ref, key_gain, query_gain, space_ref, time_ref,
    *others,
):
    held = len(others) - HELD_BEHIND
    shared, (out_ref, *gathered) = others[: held // 2], others[held // 2 : held + 1]
    (
        state, row_in, mine, before, final, hidden,
        rs_send, rs_recv, p_send, p_recv, g_send, g_recv, h_send, h_recv,
        own_sem, line_send, side_send, pair_send, full_recv, kv_send, kv_recv,
    ) = others[held + 1 :]
    me_t, me_r = lax.axis_index("tm"), lax.axis_index("row")
    width = key_ref.shape[1]
    groups = groups_of(width)
    per_part = -(-len(groups) // count_r)

    barrier = pltpu.get_barrier_semaphore()

    def greet_t(k, carry):
        pl.semaphore_signal(
            barrier, inc=1, device_id={"tm": lax.rem(me_t + k, count_t)}, device_id_type=MESH
        )
        return carry

    lax.fori_loop(1, count_t, greet_t, 0)
    for k in range(1, count_r):
        pl.semaphore_signal(
            barrier, inc=1, device_id={"row": lax.rem(me_r + k, count_r)}, device_id_type=MESH
        )

    kv_in, kv_out = shared[:2], gathered[:2]
    w_in, w_out = shared[2:], gathered[2:]
    sent_copies = []
    own_copies = []

    def w_slot(a, r, t):
        return w_out[a].at[r, t] if a == 0 else w_out[a].at[t, r]

    def kv_slot(a, r):
        return kv_out[a].at[:, r]

    def run(condition, action):
        if condition is None:
            action()
        else:
            pl.when(condition)(action)

    def send(condition, source, target, send_sem, recv_sem, device):
        def copy():
            return pltpu.make_async_remote_copy(
                src_ref=source(), dst_ref=target(), send_sem=send_sem(), recv_sem=recv_sem(),
                device_id=device, device_id_type=MESH,
            )

        run(condition, lambda: copy().start())
        sent_copies.append((condition, lambda: copy().wait_send()))

    def arrive(condition, slot, recv_sem):
        def wait():
            pltpu.make_async_remote_copy(
                src_ref=slot(), dst_ref=slot(), send_sem=own_sem.at[0], recv_sem=recv_sem(),
                device_id={"row": lax.rem(me_r + 1, count_r)}, device_id_type=MESH,
            ).wait_recv()

        run(condition, wait)

    def reach(d):
        if d == 0:
            return [(None, me_r)]
        return [(me_r >= d, me_r - d), (me_r < count_r - d, me_r + d)]

    def both(first, second):
        return second if first is None else jnp.logical_and(first, second)

    def onward(d, a, source, slot, sems, recv):
        for index, (valid, r) in enumerate(reach(d)):
            for step in (-1, 1) if d == 0 else ((1,) if index == 0 else (-1,)):
                inside = (me_r < count_r - 1) if step > 0 else (me_r > 0)
                lane = (step + 1) // 2
                send(
                    both(valid, inside),
                    lambda a=a, r=r: source(a, r),
                    lambda a=a, r=r: slot(a, r),
                    lambda a=a, r=r, lane=lane: sems.at[a, r, lane],
                    lambda a=a, r=r: recv(a, r),
                    {"row": me_r + step},
                )

    flip = lambda bits: lax.bitwise_xor(me_t, jnp.int32(bits))

    def pair(valid, a, r, t, source):
        send(
            valid, source, lambda: w_slot(a, r, t), lambda: pair_send.at[a, r, t],
            lambda: full_recv.at[a, r, t], {"tm": flip(1)},
        )

    def weights_line(d):
        def source(a, r):
            return w_in[a] if d == 0 else w_slot(a, r, me_t)

        for a in range(len(w_in)):
            if d > 0:
                for valid, r in reach(d):
                    arrive(
                        valid, lambda a=a, r=r: w_slot(a, r, me_t),
                        lambda a=a, r=r: full_recv.at[a, r, me_t],
                    )
            onward(
                d, a, source, lambda a, r: w_slot(a, r, me_t), line_send,
                lambda a, r: full_recv.at[a, r, me_t],
            )
            for valid, r in reach(d):
                for side, bits in ((0, 2), (1, 4)):
                    send(
                        valid,
                        lambda a=a, r=r: source(a, r),
                        lambda a=a, r=r: w_slot(a, r, me_t),
                        lambda a=a, r=r, side=side: side_send.at[a, r, side, 0],
                        lambda a=a, r=r: full_recv.at[a, r, me_t],
                        {"tm": flip(bits)},
                    )
                pair(valid, a, r, me_t, lambda a=a, r=r: source(a, r))

    def weights_plane(d):
        for a in range(len(w_in)):
            for valid, r in reach(d):
                for side, bits, other in ((1, 2, 4), (0, 4, 2)):
                    t = flip(bits)
                    slot = lambda a=a, r=r, t=t: w_slot(a, r, t)
                    recv = lambda a=a, r=r, t=t: full_recv.at[a, r, t]
                    arrive(valid, slot, recv)
                    send(
                        both(valid, lax.rem(r, 2) == 1 - side), slot, slot,
                        lambda a=a, r=r, side=side: side_send.at[a, r, side, 1],
                        recv, {"tm": flip(other)},
                    )
                    pair(valid, a, r, t, slot)

    def weights_corner(d):
        for a in range(len(w_in)):
            for valid, r in reach(d):
                t = flip(6)
                slot = lambda a=a, r=r, t=t: w_slot(a, r, t)
                arrive(valid, slot, lambda a=a, r=r, t=t: full_recv.at[a, r, t])
                pair(valid, a, r, t, slot)

    def weights_rest():
        for a in range(len(w_in)):
            for r in range(count_r):
                for bits in (1, 3, 5, 7):
                    t = flip(bits)
                    arrive(
                        None, lambda a=a, r=r, t=t: w_slot(a, r, t),
                        lambda a=a, r=r, t=t: full_recv.at[a, r, t],
                    )

    def targets_line(d):
        def source(a, r):
            return kv_in[a] if d == 0 else kv_slot(a, r)

        for a in range(2):
            if d > 0:
                for valid, r in reach(d):
                    arrive(
                        valid, lambda a=a, r=r: kv_slot(a, r), lambda a=a, r=r: kv_recv.at[a, r]
                    )
            onward(d, a, source, kv_slot, kv_send, lambda a, r: kv_recv.at[a, r])

    for a in range(2):
        own_copies.append((kv_in[a], kv_slot(a, me_r)))
    for a in range(len(w_in)):
        own_copies.append((w_in[a], w_slot(a, me_r, me_t)))
    own_copies = [
        pltpu.make_async_copy(source, target, own_sem.at[i])
        for i, (source, target) in enumerate(own_copies)
    ]
    for copy in own_copies:
        copy.start()
    pl.semaphore_wait(barrier, count_t - 1 + count_r - 1)
    weights_line(0)

    state[...] = jnp.zeros_like(state)
    for index, (start, size) in enumerate(groups):
        mask = same_head(size)
        ones = mask.astype(BF16)
        lanes = pl.ds(start, size)
        feat = features(key_ref[:, lanes], key_gain[:, lanes], ones)
        high, low = parts(feat)
        values = value_ref[:, lanes]
        outer = (token_dot(high, values) + token_dot(low, values)) * mask
        packed = outer[0:HEAD_DIM]
        for head in range(1, size // HEAD_DIM):
            packed = packed + outer[head * HEAD_DIM : (head + 1) * HEAD_DIM]
        sums = jnp.broadcast_to(jnp.sum(feat, axis=0, keepdims=True), (SLAB - HEAD_DIM, size))
        tail = lax.broadcasted_iota(jnp.int32, sums.shape, 0) == 0
        block = jnp.concatenate([packed, jnp.where(tail, sums, 0.0)], axis=0)
        state[index // per_part, :, pl.ds((index % per_part) * LANES, size)] = block.astype(
            STATE_TYPE
        )

    def row_copy(peer, slot):
        return pltpu.make_async_remote_copy(
            src_ref=state.at[peer], dst_ref=row_in.at[slot],
            send_sem=rs_send.at[peer], recv_sem=rs_recv.at[slot],
            device_id={"row": peer}, device_id_type=MESH,
        )

    for k in range(1, count_r):
        row_copy(lax.rem(me_r + k, count_r), me_r).start()
    weights_line(1)
    targets_line(0)
    total = state[me_r].astype(F32)
    for k in range(1, count_r):
        peer = lax.rem(me_r + k, count_r)
        row_copy(peer, peer).wait_recv()
        total = total + row_in[peer].astype(F32)
    mine[...] = total.astype(STATE_TYPE)

    def prefix_copy(peer, slot):
        return pltpu.make_async_remote_copy(
            src_ref=mine, dst_ref=before.at[slot],
            send_sem=p_send.at[peer], recv_sem=p_recv.at[slot],
            device_id={"tm": peer}, device_id_type=MESH,
        )

    def send_later(peer, carry):
        prefix_copy(peer, me_t).start()
        return carry

    lax.fori_loop(me_t + 1, count_t, send_later, 0)
    final[me_r] = total.astype(STATE_TYPE)

    def add_earlier(peer, carry):
        prefix_copy(peer, peer).wait_recv()
        final[me_r] = (final[me_r].astype(F32) + before[peer].astype(F32)).astype(STATE_TYPE)
        return carry

    lax.fori_loop(0, me_t, add_earlier, 0)

    def final_copy(peer, slot):
        return pltpu.make_async_remote_copy(
            src_ref=final.at[me_r], dst_ref=final.at[slot],
            send_sem=g_send.at[peer], recv_sem=g_recv.at[slot],
            device_id={"row": peer}, device_id_type=MESH,
        )

    def final_arrival(peer):
        return pltpu.make_async_remote_copy(
            src_ref=final.at[peer], dst_ref=final.at[peer],
            send_sem=g_send.at[peer], recv_sem=g_recv.at[peer],
            device_id={"row": peer}, device_id_type=MESH,
        )

    for k in range(1, count_r):
        final_copy(lax.rem(me_r + k, count_r), me_r).start()
    weights_plane(0)
    for k in range(1, count_r):
        final_arrival(lax.rem(me_r + k, count_r)).wait_recv()

    for index, (start, size) in enumerate(groups):
        mask = same_head(size)
        ones = mask.astype(BF16)
        lanes = pl.ds(start, size)
        table_in = final[index // per_part, :, pl.ds((index % per_part) * LANES, size)].astype(F32)
        feat = features(query_ref[:, lanes], query_gain[:, lanes], ones)
        high, low = parts(feat)
        table = jnp.concatenate([table_in[0:HEAD_DIM]] * (size // HEAD_DIM), axis=0) * mask
        table_high, table_low = parts(table)
        numerator = dot(high, table_high) + dot(low, table_high) + dot(high, table_low)
        denominator = head_sums(feat * table_in[HEAD_DIM : HEAD_DIM + 1], ones) + 1e-06
        mixed = latent_ref[:, lanes].astype(F32) + numerator / denominator
        for f in range(frames):
            for r in range(rows):
                at = (f * rows + r) * cols
                padded = jnp.concatenate(
                    [mixed[at : at + cols], jnp.zeros((SLAB - cols, size), F32)], axis=0
                )
                hidden[f + 1, r + 1, :, lanes] = padded.astype(BF16)

    for d in range(2, count_r):
        if d == 2:
            weights_line(d)
    weights_corner(0)
    body_f, body_r = pl.ds(1, frames), pl.ds(1, rows)
    moves = (
        ("tm", me_t, count_t, -1, hidden.at[1, body_r], hidden.at[frames + 1, body_r]),
        ("tm", me_t, count_t, 1, hidden.at[frames, body_r], hidden.at[0, body_r]),
        ("row", me_r, count_r, -1, hidden.at[body_f, 1], hidden.at[body_f, rows + 1]),
        ("row", me_r, count_r, 1, hidden.at[body_f, rows], hidden.at[body_f, 0]),
    )

    def halo(i):
        axis, me, count, step, source, target = moves[i]
        return pltpu.make_async_remote_copy(
            src_ref=source, dst_ref=target, send_sem=h_send.at[i], recv_sem=h_recv.at[i],
            device_id={axis: lax.rem(me + step + count, count)}, device_id_type=MESH,
        )

    def sends(i):
        _, me, count, step, _, _ = moves[i]
        return (me > 0) if step < 0 else (me < count - 1)

    def receives(i):
        _, me, count, step, _, _ = moves[i]
        return (me < count - 1) if step < 0 else (me > 0)

    for i in range(4):
        pl.when(sends(i))(halo(i).start)
    for i in range(4):
        target = moves[i][5]

        @pl.when(jnp.logical_not(receives(i)))
        def _():
            target[...] = jnp.zeros(target.shape, BF16)

    for i in range(4):
        pl.when(receives(i))(halo(i).wait_recv)

    weights_plane(1)
    for start, size in groups:
        lanes = pl.ds(start, size)
        taps = [space_ref[i : i + 1, lanes] for i in range(9)]
        times = [time_ref[i : i + 1, lanes] for i in range(3)]
        for f in range(frames):
            for r in range(rows):
                total = jnp.zeros((SLAB, size), F32)
                for a in range(3):
                    slab = hidden[f + 1, r + a, :, lanes].astype(F32)
                    if a == 1:
                        total = total + slab * (1.0 + times[1])
                    total = total + taps[3 * a + 1] * slab
                    total = total + taps[3 * a] * pltpu.roll(slab, 1, 0)
                    total = total + taps[3 * a + 2] * pltpu.roll(slab, SLAB - 1, 0)
                for a in (0, 2):
                    total = total + times[a] * hidden[f + a, r + 1, :, lanes].astype(F32)
                out_ref[f * rows + r, :, lanes] = total[0:cols].astype(BF16)

    for d in range(3, count_r):
        weights_line(d)
    targets_line(1)
    weights_corner(1)
    for d in range(2, count_r):
        weights_plane(d)
        targets_line(d)
        weights_corner(d)
    weights_rest()
    for copy in own_copies:
        copy.wait()
    for condition, action in sent_copies:
        run(condition, action)
    for i in range(4):
        pl.when(sends(i))(halo(i).wait_send)
    for k in range(1, count_r):
        peer = lax.rem(me_r + k, count_r)
        row_copy(peer, me_r).wait_send()
        final_copy(peer, me_r).wait_send()

    def sent(peer, carry):
        prefix_copy(peer, me_t).wait_send()
        return carry

    lax.fori_loop(me_t + 1, count_t, sent, 0)


def front(
    latent, query_raw, key_raw, value_raw, query_gain, key_gain, space_kernel, time_kernel,
    targets, weights,
):
    frames, rows, cols, width = latent.shape
    count_t, count_r = lax.axis_size("tm"), lax.axis_size("row")
    tokens = frames * rows * cols
    part = -(-len(groups_of(width)) // count_r) * LANES
    flat = lambda x: x.reshape(tokens, width)
    dma = pltpu.SemaphoreType.DMA
    vmem = pl.BlockSpec(memory_space=pltpu.VMEM)
    anywhere = pl.BlockSpec(memory_space=pl.ANY)
    shared = tuple(targets) + tuple(weights)
    kept = [(x.shape[0], count_r) + x.shape[1:] for x in targets]
    for x, lead in zip(weights, ((count_r, count_t), (count_t, count_r))):
        kept.append(lead + x.shape)
    shapes = [(frames * rows, cols, width)] + kept
    out, *full = pl.pallas_call(
        functools.partial(front_kernel, count_t, count_r, frames, rows, cols),
        out_shape=[jax.ShapeDtypeStruct(shape, BF16) for shape in shapes],
        in_specs=[vmem] * 8 + [anywhere] * len(shared),
        out_specs=[vmem] + [anywhere] * len(shared),
        scratch_shapes=[
            pltpu.VMEM((count_r, SLAB, part), STATE_TYPE),
            pltpu.VMEM((count_r, SLAB, part), STATE_TYPE),
            pltpu.VMEM((SLAB, part), STATE_TYPE),
            pltpu.VMEM((count_t, SLAB, part), STATE_TYPE),
            pltpu.VMEM((count_r, SLAB, part), STATE_TYPE),
            pltpu.VMEM((frames + 2, rows + 2, SLAB, width), BF16),
            dma((count_r,)), dma((count_r,)), dma((count_t,)), dma((count_t,)),
            dma((count_r,)), dma((count_r,)), dma((4,)), dma((4,)),
            dma((4,)), dma((2, count_r, 2)), dma((2, count_r, 2, 2)),
            dma((2, count_r, count_t)), dma((2, count_r, count_t)),
            dma((2, count_r, 2)), dma((2, count_r)),
        ],
        compiler_params=pltpu.CompilerParams(
            collective_id=0, has_side_effects=True, vmem_limit_bytes=40 * 1024 * 1024
        ),
    )(
        flat(key_raw), flat(value_raw), flat(query_raw), flat(latent),
        key_gain.reshape(1, width), query_gain.reshape(1, width),
        space_kernel.reshape(9, width), time_kernel, *shared,
    )
    return out.reshape(latent.shape), full


def per_device(
    latent, query_raw, key_raw, value_raw, query_gain, key_gain, space_kernel, time_kernel,
    first_weight, first_bias, second_weight, second_bias, target_keys, target_values,
):
    frames, rows, cols, width = latent.shape
    count_t = lax.axis_size("tm")
    gather = functools.partial(lax.all_gather, tiled=True)
    weights = (first_weight, second_weight) if count_t == CUBE else ()
    blended, (keys, values, *full) = front(
        latent, query_raw, key_raw, value_raw, query_gain, key_gain, space_kernel, time_kernel,
        (target_keys, target_values), weights,
    )
    if full:
        first_full = full[0].reshape(full[0].shape[0], width, -1)
        second_full = full[1].reshape(full[1].shape[0], -1, full[1].shape[-1])
    else:
        first_full = gather(first_weight, "tm", axis=0)
        first_full = gather(first_full, "row", axis=1)[None]
        second_full = gather(second_weight, "row", axis=0)
        second_full = gather(second_full, "tm", axis=1)[None]
    tokens = blended.reshape(-1, width)

    def layer(left, right, bias):
        product = jnp.einsum("mk,rkn->mrn", left, right, preferred_element_type=F32)
        return product.reshape(left.shape[0], -1) + bias

    units = jax.nn.silu(layer(tokens, first_full, first_bias)).astype(BF16)
    queries = layer(units, second_full, second_bias).astype(BF16)
    split = lambda x: x.reshape(frames, -1, AHEADS, AHEAD_DIM)
    scores = jnp.einsum(
        "cqgd,ckgd->cgqk", split(queries), split(keys), preferred_element_type=F32
    ) * (1.0 / AHEAD_DIM**0.5)
    weights = jnp.exp(scores - jnp.max(scores, axis=-1, keepdims=True))
    row_total = jnp.sum(weights, axis=-1)
    result = jnp.einsum(
        "cgqk,ckgd->cqgd", weights.astype(BF16), split(values), preferred_element_type=F32
    )
    result = result / jnp.transpose(row_total, (0, 2, 1))[..., None]
    attended = result.astype(BF16).reshape(frames, rows, cols, -1)
    return (blended, attended)


def solution(mesh):
    tokens = P("tm", "row", None, None)
    targets = P("tm", "row", None)
    return jax.shard_map(
        per_device,
        mesh=mesh,
        in_specs=(
            tokens, tokens, tokens, tokens, P(), P(), P(), P(),
            P("tm", "row"), P(), P("row", "tm"), P(), targets, targets,
        ),
        out_specs=(tokens, tokens),
        check_vma=False,
    )
```

```python
import functools

import jax
import jax.numpy as jnp
from jax import lax
from jax.experimental import pallas as pl
from jax.experimental.pallas import tpu as pltpu
from jax.sharding import PartitionSpec as P

HEADS = 70
HEAD_DIM = 32
AHEADS = 16
AHEAD_DIM = 80
LANES = 128
SLAB = 48
HELD_BEHIND = 27
CUBE = 8
STATE_TYPE = jnp.float32
F32, BF16 = jnp.float32, jnp.bfloat16
MESH = pl.DeviceIdType.MESH


def groups_of(width):
    return [(start, min(LANES, width - start)) for start in range(0, width, LANES)]


def same_head(size):
    row = lax.broadcasted_iota(jnp.int32, (size, size), 0) // HEAD_DIM
    col = lax.broadcasted_iota(jnp.int32, (size, size), 1) // HEAD_DIM
    return (row == col).astype(F32)


def parts(value):
    high = value.astype(BF16)
    return high, (value - high.astype(F32)).astype(BF16)


def dot(left, right):
    return jnp.dot(left, right, preferred_element_type=F32)


def token_dot(left, right):
    return lax.dot_general(left, right, (((0,), (0,)), ((), ())), preferred_element_type=F32)


def head_sums(value, ones):
    high, low = parts(value)
    return dot(high, ones) + dot(low, ones)


def features(source, gain, ones):
    values = source.astype(F32)
    mean_square = jnp.maximum(head_sums(values * values, ones) * (1.0 / HEAD_DIM), 0.25)
    return jnp.maximum(values * lax.rsqrt(mean_square) * gain, 0.0)


def front_kernel(
    count_t, count_r, frames, rows, cols,
    key_hbm, value_hbm, query_hbm, latent_hbm, key_gain, query_gain, space_ref, time_ref,
    *others,
):
    held = len(others) - HELD_BEHIND
    shared, (out_ref, *gathered) = others[: held // 2], others[held // 2 : held + 1]
    (
        state, row_in, mine, before, final, hidden,
        rs_send, rs_recv, p_send, p_recv, g_send, g_recv, h_send, h_recv,
        own_sem, line_send, side_send, pair_send, full_recv, kv_send, kv_recv,
        key_ref, value_ref, query_ref, latent_ref, load_sem,
    ) = others[held + 1 :]
    me_t, me_r = lax.axis_index("tm"), lax.axis_index("row")
    width = key_hbm.shape[1]
    loads = [
        pltpu.make_async_copy(source, target, load_sem.at[i])
        for i, (source, target) in enumerate(
            (
                (key_hbm, key_ref), (value_hbm, value_ref),
                (query_hbm, query_ref), (latent_hbm, latent_ref),
            )
        )
    ]
    for load in loads:
        load.start()
    groups = groups_of(width)
    per_part = -(-len(groups) // count_r)

    barrier = pltpu.get_barrier_semaphore()

    def greet_t(k, carry):
        pl.semaphore_signal(
            barrier, inc=1, device_id={"tm": lax.rem(me_t + k, count_t)}, device_id_type=MESH
        )
        return carry

    lax.fori_loop(1, count_t, greet_t, 0)
    for k in range(1, count_r):
        pl.semaphore_signal(
            barrier, inc=1, device_id={"row": lax.rem(me_r + k, count_r)}, device_id_type=MESH
        )

    kv_in, kv_out = shared[:2], gathered[:2]
    w_in, w_out = shared[2:], gathered[2:]
    sent_copies = []
    own_copies = []

    def w_slot(a, r, t):
        return w_out[a].at[r, t] if a == 0 else w_out[a].at[t, r]

    def kv_slot(a, r):
        return kv_out[a].at[:, r]

    def run(condition, action):
        if condition is None:
            action()
        else:
            pl.when(condition)(action)

    def send(condition, source, target, send_sem, recv_sem, device):
        def copy():
            return pltpu.make_async_remote_copy(
                src_ref=source(), dst_ref=target(), send_sem=send_sem(), recv_sem=recv_sem(),
                device_id=device, device_id_type=MESH,
            )

        run(condition, lambda: copy().start())
        sent_copies.append((condition, lambda: copy().wait_send()))

    def arrive(condition, slot, recv_sem):
        def wait():
            pltpu.make_async_remote_copy(
                src_ref=slot(), dst_ref=slot(), send_sem=own_sem.at[0], recv_sem=recv_sem(),
                device_id={"row": lax.rem(me_r + 1, count_r)}, device_id_type=MESH,
            ).wait_recv()

        run(condition, wait)

    def reach(d):
        if d == 0:
            return [(None, me_r)]
        return [(me_r >= d, me_r - d), (me_r < count_r - d, me_r + d)]

    def both(first, second):
        return second if first is None else jnp.logical_and(first, second)

    def onward(d, a, source, slot, sems, recv):
        for index, (valid, r) in enumerate(reach(d)):
            for step in (-1, 1) if d == 0 else ((1,) if index == 0 else (-1,)):
                inside = (me_r < count_r - 1) if step > 0 else (me_r > 0)
                lane = (step + 1) // 2
                send(
                    both(valid, inside),
                    lambda a=a, r=r: source(a, r),
                    lambda a=a, r=r: slot(a, r),
                    lambda a=a, r=r, lane=lane: sems.at[a, r, lane],
                    lambda a=a, r=r: recv(a, r),
                    {"row": me_r + step},
                )

    flip = lambda bits: lax.bitwise_xor(me_t, jnp.int32(bits))

    def pair(valid, a, r, t, source):
        send(
            valid, source, lambda: w_slot(a, r, t), lambda: pair_send.at[a, r, t],
            lambda: full_recv.at[a, r, t], {"tm": flip(1)},
        )

    def weights_line(d):
        def source(a, r):
            return w_in[a] if d == 0 else w_slot(a, r, me_t)

        for a in range(len(w_in)):
            if d > 0:
                for valid, r in reach(d):
                    arrive(
                        valid, lambda a=a, r=r: w_slot(a, r, me_t),
                        lambda a=a, r=r: full_recv.at[a, r, me_t],
                    )
            onward(
                d, a, source, lambda a, r: w_slot(a, r, me_t), line_send,
                lambda a, r: full_recv.at[a, r, me_t],
            )
            for valid, r in reach(d):
                for side, bits in ((0, 2), (1, 4)):
                    send(
                        valid,
                        lambda a=a, r=r: source(a, r),
                        lambda a=a, r=r: w_slot(a, r, me_t),
                        lambda a=a, r=r, side=side: side_send.at[a, r, side, 0],
                        lambda a=a, r=r: full_recv.at[a, r, me_t],
                        {"tm": flip(bits)},
                    )
                pair(valid, a, r, me_t, lambda a=a, r=r: source(a, r))

    def weights_plane(d):
        for a in range(len(w_in)):
            for valid, r in reach(d):
                for side, bits, other in ((1, 2, 4), (0, 4, 2)):
                    t = flip(bits)
                    slot = lambda a=a, r=r, t=t: w_slot(a, r, t)
                    recv = lambda a=a, r=r, t=t: full_recv.at[a, r, t]
                    arrive(valid, slot, recv)
                    send(
                        both(valid, lax.rem(r, 2) == 1 - side), slot, slot,
                        lambda a=a, r=r, side=side: side_send.at[a, r, side, 1],
                        recv, {"tm": flip(other)},
                    )
                    pair(valid, a, r, t, slot)

    def weights_corner(d):
        for a in range(len(w_in)):
            for valid, r in reach(d):
                t = flip(6)
                slot = lambda a=a, r=r, t=t: w_slot(a, r, t)
                arrive(valid, slot, lambda a=a, r=r, t=t: full_recv.at[a, r, t])
                pair(valid, a, r, t, slot)

    def weights_rest():
        for a in range(len(w_in)):
            for r in range(count_r):
                for bits in (1, 3, 5, 7):
                    t = flip(bits)
                    arrive(
                        None, lambda a=a, r=r, t=t: w_slot(a, r, t),
                        lambda a=a, r=r, t=t: full_recv.at[a, r, t],
                    )

    def targets_line(d):
        def source(a, r):
            return kv_in[a] if d == 0 else kv_slot(a, r)

        for a in range(2):
            if d > 0:
                for valid, r in reach(d):
                    arrive(
                        valid, lambda a=a, r=r: kv_slot(a, r), lambda a=a, r=r: kv_recv.at[a, r]
                    )
            onward(d, a, source, kv_slot, kv_send, lambda a, r: kv_recv.at[a, r])

    for a in range(2):
        own_copies.append((kv_in[a], kv_slot(a, me_r)))
    for a in range(len(w_in)):
        own_copies.append((w_in[a], w_slot(a, me_r, me_t)))
    own_copies = [
        pltpu.make_async_copy(source, target, own_sem.at[i])
        for i, (source, target) in enumerate(own_copies)
    ]
    for copy in own_copies:
        copy.start()
    pl.semaphore_wait(barrier, count_t - 1 + count_r - 1)
    weights_line(0)
    loads[0].wait()
    loads[1].wait()

    state[...] = jnp.zeros_like(state)
    for index, (start, size) in enumerate(groups):
        mask = same_head(size)
        ones = mask.astype(BF16)
        lanes = pl.ds(start, size)
        feat = features(key_ref[:, lanes], key_gain[:, lanes], ones)
        high, low = parts(feat)
        values = value_ref[:, lanes]
        outer = (token_dot(high, values) + token_dot(low, values)) * mask
        packed = outer[0:HEAD_DIM]
        for head in range(1, size // HEAD_DIM):
            packed = packed + outer[head * HEAD_DIM : (head + 1) * HEAD_DIM]
        sums = jnp.broadcast_to(jnp.sum(feat, axis=0, keepdims=True), (SLAB - HEAD_DIM, size))
        tail = lax.broadcasted_iota(jnp.int32, sums.shape, 0) == 0
        block = jnp.concatenate([packed, jnp.where(tail, sums, 0.0)], axis=0)
        state[index // per_part, :, pl.ds((index % per_part) * LANES, size)] = block.astype(
            STATE_TYPE
        )

    def row_copy(peer, slot):
        return pltpu.make_async_remote_copy(
            src_ref=state.at[peer], dst_ref=row_in.at[slot],
            send_sem=rs_send.at[peer], recv_sem=rs_recv.at[slot],
            device_id={"row": peer}, device_id_type=MESH,
        )

    for k in range(1, count_r):
        row_copy(lax.rem(me_r + k, count_r), me_r).start()
    weights_line(1)
    targets_line(0)
    total = state[me_r].astype(F32)
    for k in range(1, count_r):
        peer = lax.rem(me_r + k, count_r)
        row_copy(peer, peer).wait_recv()
        total = total + row_in[peer].astype(F32)
    mine[...] = total.astype(STATE_TYPE)

    def prefix_copy(peer, slot):
        return pltpu.make_async_remote_copy(
            src_ref=mine, dst_ref=before.at[slot],
            send_sem=p_send.at[peer], recv_sem=p_recv.at[slot],
            device_id={"tm": peer}, device_id_type=MESH,
        )

    def send_later(peer, carry):
        prefix_copy(peer, me_t).start()
        return carry

    lax.fori_loop(me_t + 1, count_t, send_later, 0)
    final[me_r] = total.astype(STATE_TYPE)

    def add_earlier(peer, carry):
        prefix_copy(peer, peer).wait_recv()
        final[me_r] = (final[me_r].astype(F32) + before[peer].astype(F32)).astype(STATE_TYPE)
        return carry

    lax.fori_loop(0, me_t, add_earlier, 0)

    def final_copy(peer, slot):
        return pltpu.make_async_remote_copy(
            src_ref=final.at[me_r], dst_ref=final.at[slot],
            send_sem=g_send.at[peer], recv_sem=g_recv.at[slot],
            device_id={"row": peer}, device_id_type=MESH,
        )

    def final_arrival(peer):
        return pltpu.make_async_remote_copy(
            src_ref=final.at[peer], dst_ref=final.at[peer],
            send_sem=g_send.at[peer], recv_sem=g_recv.at[peer],
            device_id={"row": peer}, device_id_type=MESH,
        )

    for k in range(1, count_r):
        final_copy(lax.rem(me_r + k, count_r), me_r).start()
    weights_plane(0)
    for k in range(1, count_r):
        final_arrival(lax.rem(me_r + k, count_r)).wait_recv()

    loads[2].wait()
    loads[3].wait()
    for index, (start, size) in enumerate(groups):
        mask = same_head(size)
        ones = mask.astype(BF16)
        lanes = pl.ds(start, size)
        table_in = final[index // per_part, :, pl.ds((index % per_part) * LANES, size)].astype(F32)
        feat = features(query_ref[:, lanes], query_gain[:, lanes], ones)
        high, low = parts(feat)
        table = jnp.concatenate([table_in[0:HEAD_DIM]] * (size // HEAD_DIM), axis=0) * mask
        table_high, table_low = parts(table)
        numerator = dot(high, table_high) + dot(low, table_high) + dot(high, table_low)
        denominator = head_sums(feat * table_in[HEAD_DIM : HEAD_DIM + 1], ones) + 1e-06
        mixed = latent_ref[:, lanes].astype(F32) + numerator / denominator
        for f in range(frames):
            for r in range(rows):
                at = (f * rows + r) * cols
                padded = jnp.concatenate(
                    [mixed[at : at + cols], jnp.zeros((SLAB - cols, size), F32)], axis=0
                )
                hidden[f + 1, r + 1, :, lanes] = padded.astype(BF16)

    for d in range(2, count_r):
        if d == 2:
            weights_line(d)
    weights_corner(0)
    body_f, body_r = pl.ds(1, frames), pl.ds(1, rows)
    moves = (
        ("tm", me_t, count_t, -1, hidden.at[1, body_r], hidden.at[frames + 1, body_r]),
        ("tm", me_t, count_t, 1, hidden.at[frames, body_r], hidden.at[0, body_r]),
        ("row", me_r, count_r, -1, hidden.at[body_f, 1], hidden.at[body_f, rows + 1]),
        ("row", me_r, count_r, 1, hidden.at[body_f, rows], hidden.at[body_f, 0]),
    )

    def halo(i):
        axis, me, count, step, source, target = moves[i]
        return pltpu.make_async_remote_copy(
            src_ref=source, dst_ref=target, send_sem=h_send.at[i], recv_sem=h_recv.at[i],
            device_id={axis: lax.rem(me + step + count, count)}, device_id_type=MESH,
        )

    def sends(i):
        _, me, count, step, _, _ = moves[i]
        return (me > 0) if step < 0 else (me < count - 1)

    def receives(i):
        _, me, count, step, _, _ = moves[i]
        return (me < count - 1) if step < 0 else (me > 0)

    for i in range(4):
        pl.when(sends(i))(halo(i).start)
    for i in range(4):
        target = moves[i][5]

        @pl.when(jnp.logical_not(receives(i)))
        def _():
            target[...] = jnp.zeros(target.shape, BF16)

    for i in range(4):
        pl.when(receives(i))(halo(i).wait_recv)

    weights_plane(1)
    targets_line(1)
    for start, size in groups:
        lanes = pl.ds(start, size)
        taps = [space_ref[i : i + 1, lanes] for i in range(9)]
        times = [time_ref[i : i + 1, lanes] for i in range(3)]
        for f in range(frames):
            for r in range(rows):
                total = jnp.zeros((SLAB, size), F32)
                for a in range(3):
                    slab = hidden[f + 1, r + a, :, lanes].astype(F32)
                    if a == 1:
                        total = total + slab * (1.0 + times[1])
                    total = total + taps[3 * a + 1] * slab
                    total = total + taps[3 * a] * pltpu.roll(slab, 1, 0)
                    total = total + taps[3 * a + 2] * pltpu.roll(slab, SLAB - 1, 0)
                for a in (0, 2):
                    total = total + times[a] * hidden[f + a, r + 1, :, lanes].astype(F32)
                out_ref[f * rows + r, :, lanes] = total[0:cols].astype(BF16)

    for d in range(3, count_r):
        weights_line(d)
    for d in range(2, count_r):
        targets_line(d)
    weights_corner(1)
    for d in range(2, count_r):
        weights_plane(d)
    for d in range(2, count_r):
        weights_corner(d)
    weights_rest()
    for copy in own_copies:
        copy.wait()
    for condition, action in sent_copies:
        run(condition, action)
    for i in range(4):
        pl.when(sends(i))(halo(i).wait_send)
    for k in range(1, count_r):
        peer = lax.rem(me_r + k, count_r)
        row_copy(peer, me_r).wait_send()
        final_copy(peer, me_r).wait_send()

    def sent(peer, carry):
        prefix_copy(peer, me_t).wait_send()
        return carry

    lax.fori_loop(me_t + 1, count_t, sent, 0)


def front(
    latent, query_raw, key_raw, value_raw, query_gain, key_gain, space_kernel, time_kernel,
    targets, weights,
):
    frames, rows, cols, width = latent.shape
    count_t, count_r = lax.axis_size("tm"), lax.axis_size("row")
    tokens = frames * rows * cols
    part = -(-len(groups_of(width)) // count_r) * LANES
    flat = lambda x: x.reshape(tokens, width)
    dma = pltpu.SemaphoreType.DMA
    vmem = pl.BlockSpec(memory_space=pltpu.VMEM)
    outer = pl.BlockSpec(memory_space=pltpu.HBM)
    anywhere = pl.BlockSpec(memory_space=pl.ANY)
    shared = tuple(targets) + tuple(weights)
    kept = [(x.shape[0], count_r) + x.shape[1:] for x in targets]
    for x, lead in zip(weights, ((count_r, count_t), (count_t, count_r))):
        kept.append(lead + x.shape)
    shapes = [(frames * rows, cols, width)] + kept
    out, *full = pl.pallas_call(
        functools.partial(front_kernel, count_t, count_r, frames, rows, cols),
        out_shape=[jax.ShapeDtypeStruct(shape, BF16) for shape in shapes],
        in_specs=[outer] * 4 + [vmem] * 4 + [outer] * len(shared),
        out_specs=[vmem] + [anywhere] * len(shared),
        scratch_shapes=[
            pltpu.VMEM((count_r, SLAB, part), STATE_TYPE),
            pltpu.VMEM((count_r, SLAB, part), STATE_TYPE),
            pltpu.VMEM((SLAB, part), STATE_TYPE),
            pltpu.VMEM((count_t, SLAB, part), STATE_TYPE),
            pltpu.VMEM((count_r, SLAB, part), STATE_TYPE),
            pltpu.VMEM((frames + 2, rows + 2, SLAB, width), BF16),
            dma((count_r,)), dma((count_r,)), dma((count_t,)), dma((count_t,)),
            dma((count_r,)), dma((count_r,)), dma((4,)), dma((4,)),
            dma((4,)), dma((2, count_r, 2)), dma((2, count_r, 2, 2)),
            dma((2, count_r, count_t)), dma((2, count_r, count_t)),
            dma((2, count_r, 2)), dma((2, count_r)),
            *[pltpu.VMEM((tokens, width), BF16)] * 4, dma((4,)),
        ],
        compiler_params=pltpu.CompilerParams(
            collective_id=0, has_side_effects=True, vmem_limit_bytes=40 * 1024 * 1024
        ),
    )(
        flat(key_raw), flat(value_raw), flat(query_raw), flat(latent),
        key_gain.reshape(1, width), query_gain.reshape(1, width),
        space_kernel.reshape(9, width), time_kernel, *shared,
    )
    return out.reshape(latent.shape), full


def per_device(
    latent, query_raw, key_raw, value_raw, query_gain, key_gain, space_kernel, time_kernel,
    first_weight, first_bias, second_weight, second_bias, target_keys, target_values,
):
    frames, rows, cols, width = latent.shape
    count_t = lax.axis_size("tm")
    gather = functools.partial(lax.all_gather, tiled=True)
    weights = (first_weight, second_weight) if count_t == CUBE else ()
    blended, (keys, values, *full) = front(
        latent, query_raw, key_raw, value_raw, query_gain, key_gain, space_kernel, time_kernel,
        (target_keys, target_values), weights,
    )
    if full:
        first_full = full[0].reshape(full[0].shape[0], width, -1)
        second_full = full[1].reshape(full[1].shape[0], -1, full[1].shape[-1])
    else:
        first_full = gather(first_weight, "tm", axis=0)
        first_full = gather(first_full, "row", axis=1)[None]
        second_full = gather(second_weight, "row", axis=0)
        second_full = gather(second_full, "tm", axis=1)[None]
    tokens = blended.reshape(-1, width)

    def layer(left, right, bias):
        pieces = [dot(left, right[i]) for i in range(right.shape[0])]
        return jnp.concatenate(pieces, axis=1) + bias

    units = jax.nn.silu(layer(tokens, first_full, first_bias)).astype(BF16)
    queries = layer(units, second_full, second_bias).astype(BF16)
    split = lambda x: x.reshape(frames, -1, AHEADS, AHEAD_DIM)
    scores = jnp.einsum(
        "cqgd,ckgd->cgqk", split(queries), split(keys), preferred_element_type=F32
    ) * (1.0 / AHEAD_DIM**0.5)
    weights = jnp.exp(scores - jnp.max(scores, axis=-1, keepdims=True))
    row_total = jnp.sum(weights, axis=-1)
    result = jnp.einsum(
        "cgqk,ckgd->cqgd", weights.astype(BF16), split(values), preferred_element_type=F32
    )
    result = result / jnp.transpose(row_total, (0, 2, 1))[..., None]
    attended = result.astype(BF16).reshape(frames, rows, cols, -1)
    return (blended, attended)


def solution(mesh):
    tokens = P("tm", "row", None, None)
    targets = P("tm", "row", None)
    return jax.shard_map(
        per_device,
        mesh=mesh,
        in_specs=(
            tokens, tokens, tokens, tokens, P(), P(), P(), P(),
            P("tm", "row"), P(), P("row", "tm"), P(), targets, targets,
        ),
        out_specs=(tokens, tokens),
        check_vma=False,
    )
```
